128 devices in a mesh: lat: 4 (over z_lo, core), lon: 32 (over y, z_hi, x).
Axes of the slice: x: 4, y: 4, z: 4 (z_hi: 2, z_lo: 2; z = z_hi * 2 + z_lo), core: 2. Of those that a mesh axis runs over, the one named last changes fastest.
Arguments:
- latent: bfloat16 [4, 384, 384, 512], P(None, 'lat', 'lon'), may hold values from -6 to 6
- attention_gain: float32 [512], replicated, may hold values from 0.25 to 1.75
- triple_weight: bfloat16 [512, 1536], replicated, may hold values from -0.25 to 0.25
- head_scale: float32 [8], replicated, may hold values from 0.5 to 64, as said below
- output_weight: bfloat16 [512, 512], replicated, may hold values from -0.25 to 0.25
- feed_gain: float32 [512], replicated, may hold values from 0.25 to 1.75
- up_weight: bfloat16 [512, 2048], replicated, may hold values from -0.25 to 0.25
- down_weight: bfloat16 [2048, 512], replicated, may hold values from -0.125 to 0.125
Outputs:
- block_out: bfloat16 [4, 384, 384, 512], P(None, 'lat', 'lon')
The draws below stay inside these ranges and needn't reach their ends.
Inputs may be any that keep to these rules, and one draw needn't show every extreme that they name: `head_scale`: positive factor for each head.
All inputs are finite; a program needn't handle non-finite values.
Results may differ from the reference program's by a relative error of at most 0.0065.
The reference program's roundings to bfloat16 on the way (of `normed`, `projected`, `attn_probs`, `attended`, `feed_normed` and `activated`) count: a program that leaves them out, or rounds other values in their place, can miss the bound.
Values may be sent and summed in bfloat16 or wider, within the bound.
No kernel may reach another device: no remote copies, remote signals or barrier semaphores. Data moves between devices by JAX's collectives and lax.ppermute only.
A program may use at most 256 MiB of HBM per device.

```python
import math
import jax
import jax.numpy as jnp
from jax import lax

D = 512
HEADS = 8
FF = 2048
LEVELS = 4
WL = 2
WLAT = 6
WLON = 12
HD = 64
NLAT = 384
NLON = 384


def draw_head_scale(key, part):
    key = jax.random.fold_in(key, 7)
    upper = math.log(2.0)
    return jnp.exp(jax.random.uniform(key, (HEADS,), jnp.float32, math.log(0.5), upper))


def levels(stream_key, shape, split, least, high):
    def one(dim, blocks):
        steps = jax.random.uniform(jax.random.fold_in(jax.random.fold_in(stream_key, 6), dim), (blocks,), jnp.float32, least / len(split), high / len(split))
        return jnp.repeat(jnp.exp(steps), shape[dim] // blocks).reshape((-1,) + (1,) * (len(shape) - dim - 1))

    loudness = one(*split[0])
    for cut in split[1:]:
        loudness = loudness * one(*cut)
    return loudness


def bell_draw(key, dims, width, limit, split=(), kind=jnp.bfloat16):
    values = jax.random.normal(key, dims, jnp.float32) * width
    if len(split) > 0:
        values = levels(key, dims, split, -0.22, 0.18) * values
    return jnp.clip(values, min=-limit, max=limit).astype(kind)


def setup_inputs(seed: int = 0) -> dict:
    arg_keys = jax.random.split(jax.random.key(seed), 9)
    latent = bell_draw(arg_keys[0], (LEVELS, NLAT, NLON, D), 1.0, 6.0, ((1, 4), (2, 32)))
    attention_gain = jnp.clip(1.0 + 0.15 * jax.random.normal(arg_keys[1], (D,), jnp.float32), 0.25, 1.75)
    triple_weight = bell_draw(arg_keys[2], (D, 3 * D), D ** -0.5, 0.25)
    head_scale = draw_head_scale(jax.random.fold_in(arg_keys[8], 71), 0)
    output_weight = bell_draw(arg_keys[4], (D, D), D ** -0.5, 0.25)
    feed_gain = jnp.clip(1.0 + 0.15 * jax.random.normal(arg_keys[5], (D,), jnp.float32), 0.25, 1.75)
    up_weight = bell_draw(arg_keys[6], (D, FF), D ** -0.5, 0.25)
    down_weight = bell_draw(arg_keys[7], (FF, D), FF ** -0.5, 0.125)
    return dict(latent=latent, attention_gain=attention_gain, triple_weight=triple_weight, head_scale=head_scale, output_weight=output_weight, feed_gain=feed_gain, up_weight=up_weight, down_weight=down_weight)


epsilon = 1e-05

def layer_norm(values, scaling):
    average = lax.optimization_barrier(jnp.mean(values, axis=-1, keepdims=True))
    centred = values - average
    spread = lax.optimization_barrier(jnp.mean(centred * centred, axis=-1, keepdims=True))
    return centred * lax.rsqrt(spread + epsilon) * scaling

def window_attention(column, seam_flag, triple_weight, head_scale):
    level_wins = LEVELS // WL
    row_wins = NLAT // WLAT
    window_len = WL * WLAT * WLON
    count = level_wins * row_wins
    windows = column.reshape(level_wins, WL, row_wins, WLAT, WLON, D)
    windows = windows.transpose(0, 2, 1, 3, 4, 5).reshape(count, window_len, D)
    projected = jnp.dot(windows.reshape(-1, D), triple_weight, preferred_element_type=jnp.float32)
    projected = projected.astype(jnp.bfloat16).reshape(count, window_len, 3, HEADS, HD)
    query_part = projected[:, :, 0].astype(jnp.float32)
    key_part = projected[:, :, 1].astype(jnp.float32)
    value_part = projected[:, :, 2].astype(jnp.float32)
    scores = jnp.einsum('wqhd,wkhd->whqk', query_part, key_part)
    scores = scores * (head_scale / jnp.sqrt(jnp.float32(HD)))[None, :, None, None]
    token_flag = jnp.broadcast_to(seam_flag.reshape(1, row_wins, 1, WLAT, 1), (level_wins, row_wins, WL, WLAT, WLON))
    token_flag = token_flag.reshape(count, window_len)
    allowed = token_flag[:, :, None] == token_flag[:, None, :]
    scores = jnp.where(allowed[:, None], scores, -1e+30)
    row_max = lax.optimization_barrier(jnp.max(scores, axis=-1, keepdims=True))
    weights = jnp.exp(scores - row_max)
    attn_probs = (weights / lax.optimization_barrier(jnp.sum(weights, axis=-1, keepdims=True))).astype(jnp.bfloat16)
    attended = jnp.einsum('whqk,wkhd->wqhd', attn_probs.astype(jnp.float32), value_part).astype(jnp.bfloat16)
    attended = attended.reshape(level_wins, row_wins, WL, WLAT, WLON, D).transpose(0, 2, 1, 3, 4, 5)
    return attended.reshape(LEVELS, NLAT, WLON, D)

def reference(latent, attention_gain, triple_weight, head_scale, output_weight, feed_gain, up_weight, down_weight):
    half_lat = WLAT // 2
    half_lon = WLON // 2
    normed = layer_norm(latent.astype(jnp.float32), attention_gain).astype(jnp.bfloat16)
    rolled = jnp.roll(normed, (-half_lat, -half_lon), axis=(1, 2))
    seam_flag = (jnp.arange(NLAT, dtype=jnp.int32) + half_lat) % NLAT < half_lat
    columns = rolled.reshape(LEVELS, NLAT, NLON // WLON, WLON, D).transpose(2, 0, 1, 3, 4)
    attended = lax.map(lambda column: window_attention(column, seam_flag, triple_weight, head_scale), columns)
    attended = attended.transpose(1, 2, 0, 3, 4).reshape(LEVELS, NLAT, NLON, D)
    attended = jnp.roll(attended, (half_lat, half_lon), axis=(1, 2))

    def token_block(items):
        inputs, mixes = items
        residual = inputs.astype(jnp.float32) + jnp.dot(mixes, output_weight, preferred_element_type=jnp.float32)
        feed_normed = layer_norm(residual, feed_gain).astype(jnp.bfloat16)
        hidden = jnp.dot(feed_normed, up_weight, preferred_element_type=jnp.float32)
        activated = jax.nn.gelu(hidden, approximate=False).astype(jnp.bfloat16)
        return (residual + jnp.dot(activated, down_weight, preferred_element_type=jnp.float32)).astype(jnp.bfloat16)
    outputs = lax.map(token_block, (latent.reshape(LEVELS * NLAT, NLON, D), attended.reshape(LEVELS * NLAT, NLON, D)))
    return outputs.reshape(LEVELS, NLAT, NLON, D)
```

```python
import functools

import jax
import jax.numpy as jnp
import numpy as np
from jax import lax
from jax.experimental import pallas as pl
from jax.experimental.pallas import tpu as pltpu
from jax.sharding import PartitionSpec as P

WL = 2
WLAT = 6
WLON = 12
HALF_LAT = WLAT // 2
HALF_LON = WLON // 2
EPS = 1e-05
SLABS = 4
HALO = 16
LOG2E = 1.4426950408889634
VMEM_LIMIT = 56 * 1024 * 1024

GELU_POLY = (
    0.7978843450546265,
    0.036333974450826645,
    -3.2892232411541045e-05,
    -5.53166501049418e-05,
    3.98052634409396e-06,
    -1.342210396160226e-07,
    1.8247197086651568e-09,
)


def from_behind(shard, axis, by):
    count = lax.axis_size(axis)
    return lax.ppermute(shard, axis, [(i, (i + by) % count) for i in range(count)])


def norm_rows(values, gain):
    average = jnp.mean(values, axis=-1, keepdims=True)
    centred = values - average
    spread = jnp.mean(centred * centred, axis=-1, keepdims=True)
    return centred * lax.rsqrt(spread + EPS) * gain


def gelu(x):
    u = x * x
    p = jnp.full_like(x, GELU_POLY[-1])
    for c in GELU_POLY[-2::-1]:
        p = p * u + c
    half = 0.5 * x
    return half + half * jnp.tanh(x * p)


def gather_tables(rows):
    wins = rows // WLAT + 1
    piece = SLABS * WLAT
    half = wins // 2
    halfrows = rows // 2

    def pick(w0, w1, r0, r1, halo):
        span = r1 - r0
        table = np.zeros(((w1 - w0) * piece, SLABS * span + (SLABS * HALO if halo else 0)), np.float32)
        for w in range(w0, w1):
            for s in range(SLABS):
                for i in range(WLAT):
                    r = w * WLAT - HALF_LAT + i
                    t = (w - w0) * piece + s * WLAT + i
                    if r < 0:
                        table[t, SLABS * span + s * HALO + r + HALF_LAT] = 1
                    elif r >= rows:
                        table[t, SLABS * span + s * HALO + HALF_LAT + r - rows] = 1
                    else:
                        table[t, s * span + r - r0] = 1
        return table

    first = pick(0, half, 0, halfrows, True)
    middle = pick(half, wins - 1, halfrows - 16, rows, False)
    last = pick(wins - 1, wins, rows - 16, rows, True)

    def place(w0, w1, r0, r1):
        table = np.zeros((SLABS * (r1 - r0), (w1 - w0) * piece), np.float32)
        for s in range(SLABS):
            for r in range(r0, r1):
                w, i = divmod(r + HALF_LAT, WLAT)
                table[s * (r1 - r0) + r - r0, (w - w0) * piece + s * WLAT + i] = 1
        return table

    upper = place(0, half + 1, 0, halfrows)
    lower = place(half, wins, halfrows, rows)
    return [jnp.asarray(t, jnp.bfloat16) for t in (first, middle, last, upper, lower)]


def seam_table():
    i = np.arange(WL * WLON * WLAT) % WLAT < HALF_LAT
    return jnp.asarray(np.where(i[:, None] == i[None, :], 0.0, -1e30), jnp.float32)


def attention_kernel(
    seam_ref, factor_ref, own_ref, recv_ref, halo_own_ref, halo_recv_ref,
    first_ref, middle_ref, last_ref, upper_ref, lower_ref, bias_ref,
    gain_ref, weight_ref, att_own_ref, att_send_ref, xw_ref, aw_ref,
):
    rows, channels = own_ref.shape[2], own_ref.shape[3]
    wins = rows // WLAT + 1
    half = wins // 2
    halfrows = rows // 2
    piece = SLABS * WLAT
    tokens = WL * WLON * WLAT
    heads = factor_ref.shape[0]
    head_dim = channels // heads
    group_heads = 256 // head_dim
    groups = heads // group_heads
    slabs_half = WL * HALF_LON

    def slab(ref, s):
        return ref.at[s // HALF_LON, s % HALF_LON]

    for g in range(2 * slabs_half // SLABS):
        src, halo = (own_ref, halo_own_ref) if g * SLABS < slabs_half else (recv_ref, halo_recv_ref)
        base = g * SLABS % slabs_half
        ids = range(base, base + SLABS)
        edge = [slab(halo, s)[...] for s in ids]
        for table, r0, r1, w0, w1, use_edge in (
            (first_ref, 0, halfrows, 0, half, True),
            (middle_ref, halfrows - 16, rows, half, wins - 1, False),
            (last_ref, rows - 16, rows, wins - 1, wins, True),
        ):
            body = [slab(src, s)[r0:r1, :] for s in ids]
            stacked = jnp.concatenate(body + (edge if use_edge else []), axis=0)
            picked = jnp.dot(table[...], stacked, preferred_element_type=jnp.float32)
            for w in range(w0, w1):
                xw_ref[w, g * piece:(g + 1) * piece, :] = picked[(w - w0) * piece:(w - w0 + 1) * piece]

    lane = lax.broadcasted_iota(jnp.int32, (1, 256), 1) // head_dim
    gain = gain_ref[...]

    def window(w, bias):
        normed = norm_rows(xw_ref[w], gain).astype(jnp.bfloat16)
        projected = jnp.dot(normed, weight_ref[...], preferred_element_type=jnp.float32).astype(jnp.bfloat16)
        for g in range(groups):
            q = projected[:, g * 256:(g + 1) * 256]
            k = projected[:, channels + g * 256:channels + (g + 1) * 256]
            v = projected[:, 2 * channels + g * 256:2 * channels + (g + 1) * 256]
            mixed = jnp.zeros((tokens, 256), jnp.float32)
            for h in range(group_heads):
                mine = lane == h
                qh = q * mine.astype(jnp.bfloat16)
                scores = lax.dot_general(qh, k, (((1,), (1,)), ((), ())), preferred_element_type=jnp.float32)
                if bias is not None:
                    scores = scores + bias
                top = jnp.max(scores, axis=-1, keepdims=True)
                weights = jnp.exp2((scores - top) * factor_ref[g * group_heads + h])
                probs = (weights * (1.0 / jnp.sum(weights, axis=-1, keepdims=True))).astype(jnp.bfloat16)
                out = jnp.dot(probs, v, preferred_element_type=jnp.float32)
                mixed = jnp.where(mine, out, mixed)
            for j in range(2 * slabs_half // SLABS):
                aw_ref[j, pl.ds(pl.multiple_of(w * piece, 8), piece), g * 256:(g + 1) * 256] = mixed[j * piece:(j + 1) * piece]

    def inner(w, carry):
        window(w, None)
        return carry

    window(0, bias_ref[...] * seam_ref[0])
    lax.fori_loop(1, wins - 1, inner, 0)
    window(wins - 1, bias_ref[...] * seam_ref[1])

    for g in range(2 * slabs_half // SLABS):
        dst = att_own_ref if g * SLABS < slabs_half else att_send_ref
        base = g * SLABS % slabs_half
        for table, r0, w0, w1 in ((upper_ref, 0, 0, half + 1), (lower_ref, halfrows, half, wins)):
            source = aw_ref[g, w0 * piece:w1 * piece, :].astype(jnp.bfloat16)
            placed = jnp.dot(table[...], source, preferred_element_type=jnp.float32).astype(jnp.bfloat16)
            for n, s in enumerate(range(base, base + SLABS)):
                slab(dst, s)[r0:r0 + halfrows, :] = placed[n * halfrows:(n + 1) * halfrows]


def attention(pair, seam, factor, latent, recv, halo, halo_recv, tables, bias, gain, weight):
    levels, cols, rows, channels = latent.shape
    wins = rows // WLAT + 1
    full = lambda a: pl.BlockSpec(a.shape, lambda i, n=a.ndim: (0,) * n)
    smem = pl.BlockSpec(memory_space=pltpu.SMEM)
    own = lambda r: pl.BlockSpec((WL, HALF_LON, r, channels), lambda i: (pair, 1, 0, 0))
    other = lambda r: pl.BlockSpec((WL, HALF_LON, r, channels), lambda i: (0, 0, 0, 0))
    out = jax.ShapeDtypeStruct((WL, HALF_LON, rows, channels), jnp.bfloat16)
    return pl.pallas_call(
        attention_kernel,
        grid=(1,),
        out_shape=(out, out),
        in_specs=[smem, smem, own(rows), other(rows), own(HALO), other(HALO)]
        + [full(t) for t in tables] + [full(bias), full(gain), full(weight)],
        out_specs=(other(rows), other(rows)),
        scratch_shapes=[
            pltpu.VMEM((wins, WL * WLON * WLAT, channels), jnp.float32),
            pltpu.VMEM((WL * WLON // SLABS, wins * SLABS * WLAT, channels), jnp.float32),
        ],
        compiler_params=pltpu.CompilerParams(vmem_limit_bytes=VMEM_LIMIT),
        cost_estimate=pl.CostEstimate(flops=8_000_000_000, bytes_accessed=8_000_000, transcendentals=5_000_000),
    )(seam, factor, latent, recv, halo, halo_recv, *tables, bias, gain, weight)


def feed_kernel(att_ref, latent_ref, wo_ref, gain_ref, up_ref, down_ref, *rest):
    out_ref = rest[-1]
    channels = latent_ref.shape[-1]
    hidden = up_ref.shape[1]
    block = 512
    shape = latent_ref.shape
    att = att_ref[...].reshape(-1, channels)
    residual = latent_ref[...].reshape(-1, channels).astype(jnp.float32) + jnp.dot(
        att, wo_ref[...], preferred_element_type=jnp.float32
    )
    normed = norm_rows(residual, gain_ref[...]).astype(jnp.bfloat16)
    total = residual
    for b in range(0, hidden, block):
        act = gelu(jnp.dot(normed, up_ref[:, b:b + block], preferred_element_type=jnp.float32))
        total = total + jnp.dot(act.astype(jnp.bfloat16), down_ref[b:b + block, :], preferred_element_type=jnp.float32)
    out_ref[...] = total.astype(jnp.bfloat16).reshape(shape)


def feed(pair, side, att, latent, wo, gain, up, down, out):
    levels, cols, rows, channels = latent.shape
    step = 3
    steps = HALF_LON // step
    full = lambda a: pl.BlockSpec(a.shape, lambda i, j, n=a.ndim: (0,) * n)
    place = pl.BlockSpec((1, step, rows, channels), lambda i, j: (WL * pair + i, steps * side + j, 0, 0))
    local = pl.BlockSpec((1, step, rows, channels), lambda i, j: (i, j, 0, 0))
    operands = [att, latent, wo, gain, up, down]
    specs = [local, place, full(wo), full(gain), full(up), full(down)]
    aliases = {}
    if out is not None:
        operands.append(out)
        specs.append(pl.BlockSpec(memory_space=pl.ANY))
        aliases = {len(operands) - 1: 0}
    return pl.pallas_call(
        feed_kernel,
        grid=(WL, steps),
        out_shape=jax.ShapeDtypeStruct(latent.shape, jnp.bfloat16),
        in_specs=specs,
        out_specs=place,
        input_output_aliases=aliases,
        compiler_params=pltpu.CompilerParams(vmem_limit_bytes=VMEM_LIMIT),
        cost_estimate=pl.CostEstimate(flops=6_000_000_000, bytes_accessed=8_000_000, transcendentals=2_400_000),
    )(*operands)


def per_device(
    latent,
    attention_gain,
    triple_weight,
    head_scale,
    output_weight,
    feed_gain,
    up_weight,
    down_weight,
):
    x = latent.transpose(0, 2, 1, 3)
    levels, cols, rows, channels = x.shape
    head_dim = channels // head_scale.shape[0]
    pairs = levels // WL
    lat = lax.axis_index("lat")
    count = lax.axis_size("lat")
    seam = jnp.stack([lat == 0, lat == count - 1]).astype(jnp.float32)
    factor = head_scale * (LOG2E / head_dim ** 0.5)
    tables = gather_tables(rows)
    bias = seam_table()
    gain = attention_gain.reshape(1, -1)
    gain2 = feed_gain.reshape(1, -1)

    above = from_behind(x[:, :, rows - HALF_LAT:], "lat", 1)
    below = from_behind(x[:, :, :HALF_LAT], "lat", -1)
    edges = jnp.concatenate([above, below], axis=2)
    edges_recv = from_behind(edges[:, :HALF_LON], "lon", -1)
    pad = ((0, 0), (0, 0), (0, HALO - 2 * HALF_LAT), (0, 0))
    halo = jnp.pad(edges, pad)
    halo_recv = jnp.pad(edges_recv, pad)
    recv = [from_behind(x[WL * p:WL * p + WL, :HALF_LON], "lon", -1) for p in range(pairs)]
    out = None
    returned = []
    for p in range(pairs):
        own, send = attention(
            p, seam, factor, x, recv[p], halo, halo_recv[WL * p:WL * p + WL], tables, bias, gain, triple_weight
        )
        returned.append(from_behind(send, "lon", 1))
        out = feed(p, 1, own, x, output_weight, gain2, up_weight, down_weight, out)
    for p in range(pairs):
        out = feed(p, 0, returned[p], x, output_weight, gain2, up_weight, down_weight, out)
    return out.transpose(0, 2, 1, 3)


def solution(mesh):
    in_specs = (P(None, "lat", "lon", None), P(), P(), P(), P(), P(), P(), P())
    out_specs = P(None, "lat", "lon", None)
    return jax.shard_map(
        per_device, mesh=mesh, in_specs=in_specs, out_specs=out_specs, check_vma=False
    )
```

```python
import functools

import jax
import jax.numpy as jnp
import numpy as np
from jax import lax
from jax.experimental import pallas as pl
from jax.experimental.pallas import tpu as pltpu
from jax.sharding import PartitionSpec as P

WL = 2
WLAT = 6
WLON = 12
HALF_LAT = WLAT // 2
HALF_LON = WLON // 2
EPS = 1e-05
SLABS = 4
PIECE = SLABS * WLAT
SIDE_SLABS = WL * HALF_LON
SIDE = SIDE_SLABS * WLAT
TOKENS = 2 * SIDE
GROUPS = SIDE_SLABS // SLABS
TILE = 16
THIRD = 32
LOG2E = 1.4426950408889634
VMEM_LIMIT = 36 * 1024 * 1024


def from_behind(shard, axis, by):
    count = lax.axis_size(axis)
    return lax.ppermute(shard, axis, [(i, (i + by) % count) for i in range(count)])


def norm_rows(values, gain):
    average = jnp.mean(values, axis=-1, keepdims=True)
    centred = values - average
    spread = jnp.mean(centred * centred, axis=-1, keepdims=True)
    return centred * lax.rsqrt(spread + EPS) * gain


def gelu(x):
    half = 0.5 * x
    return half + half * lax.erf(x * 0.7071067811865476)


class Part:
    def __init__(self, half, rows):
        self.half = half
        self.rows = rows
        self.mid = rows // 2
        total = rows // WLAT + 1
        cut = total // 2
        self.bands = list(range(cut)) if half == 0 else list(range(cut, total))
        self.first_kept = THIRD // WLAT
        self.carried = cut - self.first_kept
        low, main, edge = ("low", self.mid - TILE, self.mid), ("main", half * self.mid, (half + 1) * self.mid), ("edge", 0, 0)
        if half == 0:
            self.picks = [(self.bands, [main, edge])]
            self.places = [(0, THIRD, 0, cut)]
            self.offset = 0
        else:
            self.picks = [(self.bands[:-1], [low, main]), (self.bands[-1:], [("main", rows - TILE, rows), edge])]
            self.places = [(r, r + THIRD, self.first_kept, total) for r in range(THIRD, rows, THIRD)]
            self.offset = self.carried
        self.stored = len(self.bands) + self.offset
        self.tables = [self.pick_table(b, s) for b, s in self.picks] + [self.place_table(*p)[0] for p in self.places]

    def pick_table(self, bands, segments):
        width = sum(SLABS * (r1 - r0 if name != "edge" else TILE) for name, r0, r1 in segments)
        table = np.zeros((len(bands) * PIECE, width), np.float32)
        for n, band in enumerate(bands):
            for s in range(SLABS):
                for i in range(WLAT):
                    r = band * WLAT - HALF_LAT + i
                    start = 0
                    for name, r0, r1 in segments:
                        span = TILE if name == "edge" else r1 - r0
                        if name != "edge" and r0 <= r < r1:
                            table[n * PIECE + s * WLAT + i, start + s * span + r - r0] = 1
                        elif name == "edge" and r < 0:
                            table[n * PIECE + s * WLAT + i, start + s * span + r + HALF_LAT] = 1
                        elif name == "edge" and r >= self.rows:
                            table[n * PIECE + s * WLAT + i, start + s * span + r - self.rows + HALF_LAT] = 1
                        start += SLABS * span
        return jnp.asarray(table, jnp.bfloat16)

    def place_table(self, r0, r1, base, end):
        b0, b1 = (r0 + HALF_LAT) // WLAT, (r1 - 1 + HALF_LAT) // WLAT + 1
        table = np.zeros((SLABS * (r1 - r0), (b1 - b0) * PIECE), np.float32)
        for s in range(SLABS):
            for r in range(r0, r1):
                band, i = divmod(r + HALF_LAT, WLAT)
                table[s * (r1 - r0) + r - r0, (band - b0) * PIECE + s * WLAT + i] = 1
        return jnp.asarray(table, jnp.bfloat16), b0 - base, b1 - base


def seam_table():
    i = np.arange(TOKENS) % WLAT < HALF_LAT
    return jnp.asarray(np.where(i[:, None] == i[None, :], 0.0, -1e30), jnp.float32)


def block_kernel(part, pair, aliased, *refs):
    refs = list(refs)
    pop = lambda: refs.pop(0)
    seam_ref, factor_ref = pop(), pop()
    source = {name: (pop(), pop(), pop()) for name in (("main", "edge") if part.half == 0 else ("main", "edge", "low"))}
    pick_refs = [pop() for _ in part.picks]
    place_refs = [pop() for _ in part.places]
    bias_ref, gain_ref, gain2_ref = pop(), pop(), pop()
    carry_in = pop() if part.half == 1 else None
    weights_hbm = [pop() for _ in range(4)]
    if aliased:
        pop()
    out_ref = pop()
    carry_out = pop() if part.half == 0 else None
    weights = [pop() for _ in range(4)]
    xw_ref, hw_ref, att_ref, yw_ref, ow_ref, wsem, osem = refs
    qkv_ref, wo_ref, up_ref, down_ref = weights
    channels = xw_ref.shape[-1]
    heads = factor_ref.shape[0]
    head_dim = channels // heads
    group_heads = 256 // head_dim
    count = len(part.bands)
    main0 = part.half * part.mid

    copies = [pltpu.make_async_copy(a, b, wsem.at[i]) for i, (a, b) in enumerate(zip(weights_hbm, weights))]
    for copy in copies:
        copy.start()

    for dest, side in ((xw_ref, 0), (xw_ref, 1), (hw_ref, 0), (hw_ref, 1)):
        own = dest is xw_ref

        def rows_of(name, s, r0, r1):
            ref = source[name][0 if own else 1 + side]
            col = s % HALF_LON + (side * HALF_LON if own else 0)
            base = {"main": main0, "low": part.mid - TILE, "edge": 0}[name]
            if name == "edge":
                r0, r1 = 0, TILE
            return ref[s // HALF_LON, col, r0 - base:r1 - base, :]

        for g in range(GROUPS):
            ids = range(g * SLABS, (g + 1) * SLABS)
            for table, (bands, segments) in zip(pick_refs, part.picks):
                stacked = jnp.concatenate([rows_of(n, s, r0, r1) for n, r0, r1 in segments for s in ids], axis=0)
                picked = jnp.dot(table[...], stacked, preferred_element_type=jnp.float32)
                for n, band in enumerate(bands):
                    at = (side * GROUPS + g) * PIECE
                    dest[band - part.bands[0], at:at + PIECE, :] = picked[n * PIECE:(n + 1) * PIECE]

    lane = lax.broadcasted_iota(jnp.int32, (1, 256), 1) // head_dim
    gain, gain2 = gain_ref[...], gain2_ref[...]
    copies[0].wait()

    def attend(b, bias):
        normed = norm_rows(xw_ref[b], gain).astype(jnp.bfloat16)
        around = norm_rows(hw_ref[b], gain).astype(jnp.bfloat16)
        mine = jnp.dot(normed, qkv_ref[...], preferred_element_type=jnp.float32)
        other = jnp.dot(around, qkv_ref[:, channels:], preferred_element_type=jnp.float32)
        for g in range(heads // group_heads):
            at = g * 256
            mixed = []
            for side in (0, 1):
                rows = slice(side * SIDE, (side + 1) * SIDE)
                q = mine[rows, at:at + 256]
                k, v = [
                    jnp.concatenate(
                        [mine[rows, c * channels + at:c * channels + at + 256],
                         other[rows, (c - 1) * channels + at:(c - 1) * channels + at + 256]], axis=0
                    ).astype(jnp.bfloat16)
                    for c in (1, 2)
                ]
                stacked = jnp.concatenate([jnp.where(lane == h, q, 0.0) for h in range(group_heads)], axis=0)
                scores = lax.dot_general(
                    stacked.astype(jnp.bfloat16), k, (((1,), (1,)), ((), ())), preferred_element_type=jnp.float32
                )
                probs = []
                for h in range(group_heads):
                    s = scores[h * SIDE:(h + 1) * SIDE]
                    if bias is not None:
                        s = s + bias[:SIDE]
                    top = jnp.max(s, axis=-1, keepdims=True)
                    e = jnp.exp2((s - top) * factor_ref[g * group_heads + h])
                    probs.append(e * (1.0 / jnp.sum(e, axis=-1, keepdims=True)))
                probs = jnp.concatenate(probs, axis=0).astype(jnp.bfloat16)
                out = jnp.dot(probs, v, preferred_element_type=jnp.float32)
                total = out[:SIDE]
                for h in range(1, group_heads):
                    total = jnp.where(lane == h, out[h * SIDE:(h + 1) * SIDE], total)
                mixed.append(total)
            att_ref[b, :, at:at + 256] = jnp.concatenate(mixed, axis=0).astype(jnp.bfloat16)

    def feed(b):
        residual = xw_ref[b] + jnp.dot(att_ref[b], wo_ref[...], preferred_element_type=jnp.float32)
        normed = norm_rows(residual, gain2).astype(jnp.bfloat16)
        acts = gelu(jnp.dot(normed, up_ref[...], preferred_element_type=jnp.float32)).astype(jnp.bfloat16)
        result = residual + jnp.dot(acts, down_ref[...], preferred_element_type=jnp.float32)
        at = (b + part.offset) * PIECE
        at = at if isinstance(b, int) else pl.multiple_of(at, 8)
        for g in range(2 * GROUPS):
            yw_ref[g, pl.ds(at, PIECE), :] = result[g * PIECE:(g + 1) * PIECE]

    bias = bias_ref[...] * seam_ref[part.half]
    if part.half == 0:
        attend(0, bias)
    else:
        attend(0, None)
    for copy in copies[1:]:
        copy.wait()
    if part.half == 1:
        for g in range(2 * GROUPS):
            yw_ref[g, :part.carried * PIECE, :] = carry_in[g]

    def step(b, carry):
        feed(b - 1)
        attend(b, None)
        return carry

    if part.half == 0:
        lax.fori_loop(1, count, step, 0)
    else:
        lax.fori_loop(1, count - 1, step, 0)
        feed(count - 2)
        attend(count - 1, bias)
    feed(count - 1)

    for table, spec in zip(place_refs, part.places):
        r0, r1 = spec[:2]
        b0, b1 = (r0 + HALF_LAT) // WLAT, (r1 - 1 + HALF_LAT) // WLAT + 1
        for g in range(2 * GROUPS):
            band_rows = yw_ref[g, (b0 - spec[2]) * PIECE:(b1 - spec[2]) * PIECE, :].astype(jnp.bfloat16)
            placed = jnp.dot(table[...], band_rows, preferred_element_type=jnp.float32).astype(jnp.bfloat16)
            for n in range(SLABS):
                s = g % GROUPS * SLABS + n
                col = s % HALF_LON + g // GROUPS * HALF_LON
                ow_ref[s // HALF_LON, col, r0 - part.places[0][0]:r1 - part.places[0][0], :] = placed[n * THIRD:(n + 1) * THIRD]
    if carry_out is not None:
        for g in range(2 * GROUPS):
            carry_out[g] = yw_ref[g, part.first_kept * PIECE:(part.first_kept + part.carried) * PIECE, :]
    copy = pltpu.make_async_copy(
        ow_ref,
        out_ref.at[pl.ds(WL * pair, WL), :, pl.ds(part.places[0][0], ow_ref.shape[2]), :],
        osem,
    )
    copy.start()
    copy.wait()


def block(part, pair, seam, factor, x, pieces, edges, bias, gains, carry, weights, out):
    levels, cols, rows, channels = x.shape
    mid, half = part.mid, part.half
    whole = lambda a: pl.BlockSpec(a.shape, lambda i, n=a.ndim: (0,) * n)
    smem = pl.BlockSpec(memory_space=pltpu.SMEM)
    hbm = pl.BlockSpec(memory_space=pl.ANY)
    spec = lambda n, r, p, at: pl.BlockSpec((WL, n, r, channels), lambda i: (p, 0, at, 0))
    operands = [seam, factor]
    specs = [smem, smem]
    operands += [x, *pieces[half]]
    specs += [spec(cols, mid, pair, half), spec(HALF_LON, mid, 0, 0), spec(HALF_LON, mid, 0, 0)]
    operands += edges
    specs += [spec(cols, TILE, pair, 0), spec(HALF_LON, TILE, pair, 0), spec(HALF_LON, TILE, pair, 0)]
    if half == 1:
        at = mid // TILE - 1
        operands += [x, *pieces[0]]
        specs += [spec(cols, TILE, pair, at), spec(HALF_LON, TILE, 0, at), spec(HALF_LON, TILE, 0, at)]
    small = [*part.tables, bias, *gains] + ([carry] if half == 1 else [])
    operands += small
    specs += [whole(a) for a in small]
    operands += weights
    specs += [hbm] * len(weights)
    aliases = {}
    if out is not None:
        aliases = {len(operands): 0}
        operands.append(out)
        specs.append(hbm)
    shape = jax.ShapeDtypeStruct(x.shape, jnp.bfloat16)
    if half == 0:
        kept = jax.ShapeDtypeStruct((2 * GROUPS, part.carried * PIECE, channels), jnp.float32)
        out_shape, out_specs = (shape, kept), (hbm, whole(kept))
    else:
        out_shape, out_specs = shape, hbm
    count = len(part.bands)
    return pl.pallas_call(
        functools.partial(block_kernel, part, pair, out is not None),
        grid=(1,),
        out_shape=out_shape,
        in_specs=specs,
        out_specs=out_specs,
        scratch_shapes=[pltpu.VMEM(w.shape, w.dtype) for w in weights]
        + [
            pltpu.VMEM((count, TOKENS, channels), jnp.float32),
            pltpu.VMEM((count, TOKENS, channels), jnp.float32),
            pltpu.VMEM((count, TOKENS, channels), jnp.bfloat16),
            pltpu.VMEM((2 * GROUPS, part.stored * PIECE, channels), jnp.float32),
            pltpu.VMEM((WL, cols, THIRD * len(part.places), channels), jnp.bfloat16),
            pltpu.SemaphoreType.DMA((len(weights),)),
            pltpu.SemaphoreType.DMA,
        ],
        input_output_aliases=aliases,
        compiler_params=pltpu.CompilerParams(vmem_limit_bytes=VMEM_LIMIT),
        cost_estimate=pl.CostEstimate(flops=12_000_000_000, bytes_accessed=14_000_000, transcendentals=4_000_000),
    )(*operands)


def per_device(
    latent,
    attention_gain,
    triple_weight,
    head_scale,
    output_weight,
    feed_gain,
    up_weight,
    down_weight,
):
    x = latent.transpose(0, 2, 1, 3)
    levels, cols, rows, channels = x.shape
    head_dim = channels // head_scale.shape[0]
    pairs = levels // WL
    mid = rows // 2
    lat = lax.axis_index("lat")
    count = lax.axis_size("lat")
    seam = jnp.stack([lat == 0, lat == count - 1]).astype(jnp.float32)
    factor = head_scale * (LOG2E / head_dim ** 0.5)
    parts = [Part(half, rows) for half in (0, 1)]
    bias = seam_table()
    gains = [attention_gain.reshape(1, -1), feed_gain.reshape(1, -1)]
    weights = [triple_weight, output_weight, up_weight, down_weight]

    above = from_behind(x[:, :, rows - HALF_LAT:], "lat", 1)
    below = from_behind(x[:, :, :HALF_LAT], "lat", -1)
    edges = jnp.concatenate([above, below], axis=2)
    edge_left = from_behind(edges[:, HALF_LON:], "lon", 1)
    edge_right = from_behind(edges[:, :HALF_LON], "lon", -1)
    pad = ((0, 0), (0, 0), (0, TILE - 2 * HALF_LAT), (0, 0))
    edges = [jnp.pad(e, pad) for e in (edges, edge_left, edge_right)]

    out, previous = None, None
    pieces = []
    for p in range(pairs):
        for half in (0, 1):
            level, span = slice(WL * p, WL * p + WL), slice(half * mid, half * mid + mid)
            left, right = x[level, HALF_LON:, span], x[level, :HALF_LON, span]
            if previous is not None:
                left, right, *previous = lax.optimization_barrier((left, right, *previous))
            previous = [from_behind(left, "lon", 1), from_behind(right, "lon", -1)]
            pieces.append(previous)
    for p in range(pairs):
        local = pieces[2 * p:2 * p + 2]
        out, carry = block(parts[0], p, seam, factor, x, local, edges, bias, gains, None, weights, out)
        out = block(parts[1], p, seam, factor, x, local, edges, bias, gains, carry, weights, out)
    return out.transpose(0, 2, 1, 3)


def solution(mesh):
    in_specs = (P(None, "lat", "lon", None), P(), P(), P(), P(), P(), P(), P())
    out_specs = P(None, "lat", "lon", None)
    return jax.shard_map(
        per_device, mesh=mesh, in_specs=in_specs, out_specs=out_specs, check_vma=False
    )
```

```python
import functools

import jax
import jax.numpy as jnp
import numpy as np
from jax import lax
from jax.experimental import pallas as pl
from jax.experimental.pallas import tpu as pltpu
from jax.sharding import PartitionSpec as P

WL = 2
WLAT = 6
WLON = 12
HALF_LAT = WLAT // 2
HALF_LON = WLON // 2
EPS = 1e-05
SLABS = 4
PIECE = SLABS * WLAT
SIDE_SLABS = WL * HALF_LON
SIDE = SIDE_SLABS * WLAT
TOKENS = 2 * SIDE
GROUPS = SIDE_SLABS // SLABS
TILE = 16
THIRD = 32
LOG2E = 1.4426950408889634
VMEM_LIMIT = 44 * 1024 * 1024


def from_behind(shard, axis, by):
    count = lax.axis_size(axis)
    return lax.ppermute(shard, axis, [(i, (i + by) % count) for i in range(count)])


def norm_rows(values, gain):
    average = jnp.mean(values, axis=-1, keepdims=True)
    centred = values - average
    spread = jnp.mean(centred * centred, axis=-1, keepdims=True)
    return centred * lax.rsqrt(spread + EPS) * gain


def gelu(x):
    half = 0.5 * x
    return half + half * lax.erf(x * 0.7071067811865476)


class Plan:
    def __init__(self, rows):
        self.rows = rows
        self.count = rows // WLAT + 1
        half = rows // 2
        cut = self.count // 2
        edge = ("edge", 0, 0)
        self.picks = [
            (range(cut), [("main", 0, half), edge]),
            (range(cut, self.count - 1), [("main", half - TILE, rows)]),
            (range(self.count - 1, self.count), [("main", rows - TILE, rows), edge]),
        ]
        self.places = [(r, r + THIRD) for r in range(0, rows, THIRD)]
        self.tables = [self.pick_table(*p) for p in self.picks] + [self.place_table(*p) for p in self.places]

    def bands_of(self, r0, r1):
        return (r0 + HALF_LAT) // WLAT, (r1 - 1 + HALF_LAT) // WLAT + 1

    def pick_table(self, bands, segments):
        width = sum(SLABS * (r1 - r0 if name != "edge" else TILE) for name, r0, r1 in segments)
        table = np.zeros((len(bands) * PIECE, width), np.float32)
        for n, band in enumerate(bands):
            for s in range(SLABS):
                for i in range(WLAT):
                    r = band * WLAT - HALF_LAT + i
                    start = 0
                    for name, r0, r1 in segments:
                        span = TILE if name == "edge" else r1 - r0
                        if name != "edge" and r0 <= r < r1:
                            table[n * PIECE + s * WLAT + i, start + s * span + r - r0] = 1
                        elif name == "edge" and r < 0:
                            table[n * PIECE + s * WLAT + i, start + s * span + r + HALF_LAT] = 1
                        elif name == "edge" and r >= self.rows:
                            table[n * PIECE + s * WLAT + i, start + s * span + r - self.rows + TILE // 2] = 1
                        start += SLABS * span
        return jnp.asarray(table, jnp.bfloat16)

    def place_table(self, r0, r1):
        b0, b1 = self.bands_of(r0, r1)
        table = np.zeros((SLABS * (r1 - r0), (b1 - b0) * PIECE), np.float32)
        for s in range(SLABS):
            for r in range(r0, r1):
                band, i = divmod(r + HALF_LAT, WLAT)
                table[s * (r1 - r0) + r - r0, (band - b0) * PIECE + s * WLAT + i] = 1
        return jnp.asarray(table, jnp.bfloat16)


def seam_table():
    i = np.arange(TOKENS) % WLAT < HALF_LAT
    return jnp.asarray(np.where(i[:, None] == i[None, :], 0.0, -1e30), jnp.float32)


def block_kernel(plan, pair, aliased, *refs):
    refs = list(refs)
    pop = lambda: refs.pop(0)
    seam_ref, factor_ref = pop(), pop()
    own_ref, around_refs, edge_ref = pop(), (pop(), pop()), pop()
    pick_refs = [pop() for _ in plan.picks]
    place_refs = [pop() for _ in plan.places]
    bias_ref, gain_ref, gain2_ref = pop(), pop(), pop()
    weights_hbm = [pop() for _ in range(4)]
    if aliased:
        pop()
    out_ref = pop()
    weights = [pop() for _ in range(4)]
    xw_ref, hw_ref, att_ref, yw_ref, ow_ref, wsem, osem = refs
    qkv_ref, wo_ref, up_ref, down_ref = weights
    channels = xw_ref.shape[-1]
    heads = factor_ref.shape[0]
    head_dim = channels // heads
    group_heads = 256 // head_dim
    count = plan.count

    copies = [pltpu.make_async_copy(a, b, wsem.at[i]) for i, (a, b) in enumerate(zip(weights_hbm, weights))]
    for copy in copies:
        copy.start()

    for dest, side in ((xw_ref, 0), (xw_ref, 1), (hw_ref, 0), (hw_ref, 1)):
        own = dest is xw_ref

        def rows_of(name, s, r0, r1):
            level, col = s // HALF_LON, s % HALF_LON + (side * HALF_LON if own else 0)
            if name == "edge":
                return edge_ref[level, col] if own else around_refs[side][level, col, plan.rows:plan.rows + TILE, :]
            ref = own_ref if own else around_refs[side]
            return ref[level, col, r0:r1, :]

        for g in range(GROUPS):
            ids = range(g * SLABS, (g + 1) * SLABS)
            at = (side * GROUPS + g) * PIECE
            for table, (bands, segments) in zip(pick_refs, plan.picks):
                stacked = jnp.concatenate([rows_of(n, s, r0, r1) for n, r0, r1 in segments for s in ids], axis=0)
                picked = jnp.dot(table[...], stacked, preferred_element_type=jnp.float32)
                for n, band in enumerate(bands):
                    dest[band, at:at + PIECE, :] = picked[n * PIECE:(n + 1) * PIECE]

    lane = lax.broadcasted_iota(jnp.int32, (1, 256), 1) // head_dim
    gain, gain2 = gain_ref[...], gain2_ref[...]
    copies[0].wait()

    def attend(b, bias):
        normed = norm_rows(xw_ref[b], gain).astype(jnp.bfloat16)
        around = norm_rows(hw_ref[b], gain).astype(jnp.bfloat16)
        mine = jnp.dot(normed, qkv_ref[...], preferred_element_type=jnp.float32)
        other = jnp.dot(around, qkv_ref[:, channels:], preferred_element_type=jnp.float32)
        for g in range(heads // group_heads):
            at = g * 256
            mixed = []
            for side in (0, 1):
                rows = slice(side * SIDE, (side + 1) * SIDE)
                q = mine[rows, at:at + 256]
                k, v = [
                    jnp.concatenate(
                        [mine[rows, c * channels + at:c * channels + at + 256],
                         other[rows, (c - 1) * channels + at:(c - 1) * channels + at + 256]], axis=0
                    ).astype(jnp.bfloat16)
                    for c in (1, 2)
                ]
                stacked = jnp.concatenate([jnp.where(lane == h, q, 0.0) for h in range(group_heads)], axis=0)
                scores = lax.dot_general(
                    stacked.astype(jnp.bfloat16), k, (((1,), (1,)), ((), ())), preferred_element_type=jnp.float32
                )
                probs = []
                for h in range(group_heads):
                    s = scores[h * SIDE:(h + 1) * SIDE]
                    if bias is not None:
                        s = s + bias[:SIDE]
                    top = jnp.max(s, axis=-1, keepdims=True)
                    e = jnp.exp2((s - top) * factor_ref[g * group_heads + h])
                    probs.append(e * (1.0 / jnp.sum(e, axis=-1, keepdims=True)))
                probs = jnp.concatenate(probs, axis=0).astype(jnp.bfloat16)
                out = jnp.dot(probs, v, preferred_element_type=jnp.float32)
                total = out[:SIDE]
                for h in range(1, group_heads):
                    total = jnp.where(lane == h, out[h * SIDE:(h + 1) * SIDE], total)
                mixed.append(total)
            att_ref[b, :, at:at + 256] = jnp.concatenate(mixed, axis=0).astype(jnp.bfloat16)

    def feed(b):
        residual = xw_ref[b] + jnp.dot(att_ref[b], wo_ref[...], preferred_element_type=jnp.float32)
        normed = norm_rows(residual, gain2).astype(jnp.bfloat16)
        acts = gelu(jnp.dot(normed, up_ref[...], preferred_element_type=jnp.float32)).astype(jnp.bfloat16)
        result = residual + jnp.dot(acts, down_ref[...], preferred_element_type=jnp.float32)
        at = b * PIECE
        at = at if isinstance(b, int) else pl.multiple_of(at, 8)
        for g in range(2 * GROUPS):
            yw_ref[g, pl.ds(at, PIECE), :] = result[g * PIECE:(g + 1) * PIECE]

    attend(0, bias_ref[...] * seam_ref[0])
    for copy in copies[1:]:
        copy.wait()

    def step(b, carry):
        feed(b - 1)
        attend(b, None)
        return carry

    lax.fori_loop(1, count - 1, step, 0)
    feed(count - 2)
    attend(count - 1, bias_ref[...] * seam_ref[1])
    feed(count - 1)

    for table, (r0, r1) in zip(place_refs, plan.places):
        b0, b1 = plan.bands_of(r0, r1)
        for g in range(2 * GROUPS):
            band_rows = yw_ref[g, b0 * PIECE:b1 * PIECE, :].astype(jnp.bfloat16)
            placed = jnp.dot(table[...], band_rows, preferred_element_type=jnp.float32).astype(jnp.bfloat16)
            for n in range(SLABS):
                s = g % GROUPS * SLABS + n
                col = s % HALF_LON + g // GROUPS * HALF_LON
                ow_ref[s // HALF_LON, col, r0:r1, :] = placed[n * THIRD:(n + 1) * THIRD]
    copy = pltpu.make_async_copy(ow_ref, out_ref.at[pl.ds(WL * pair, WL)], osem)
    copy.start()
    copy.wait()


def block(plan, pair, seam, factor, x, around, edges, bias, gains, weights, out):
    levels, cols, rows, channels = x.shape
    once = pl.Buffered(1)
    whole = lambda a: pl.BlockSpec(a.shape, lambda i, n=a.ndim: (0,) * n, pipeline_mode=once)
    smem = pl.BlockSpec(memory_space=pltpu.SMEM)
    hbm = pl.BlockSpec(memory_space=pl.ANY)
    mine = lambda r: pl.BlockSpec((WL, cols, r, channels), lambda i: (pair, 0, 0, 0), pipeline_mode=once)
    small = [*plan.tables, bias, *gains]
    operands = [seam, factor, x, *around, edges, *small, *weights]
    specs = [smem, smem, mine(rows), whole(around[0]), whole(around[1]), mine(TILE)]
    specs += [whole(a) for a in small] + [hbm] * len(weights)
    aliases = {}
    if out is not None:
        aliases = {len(operands): 0}
        operands.append(out)
        specs.append(hbm)
    return pl.pallas_call(
        functools.partial(block_kernel, plan, pair, out is not None),
        grid=(1,),
        out_shape=jax.ShapeDtypeStruct(x.shape, jnp.bfloat16),
        in_specs=specs,
        out_specs=hbm,
        scratch_shapes=[pltpu.VMEM(w.shape, w.dtype) for w in weights]
        + [
            pltpu.VMEM((plan.count, TOKENS, channels), jnp.float32),
            pltpu.VMEM((plan.count, TOKENS, channels), jnp.float32),
            pltpu.VMEM((plan.count, TOKENS, channels), jnp.bfloat16),
            pltpu.VMEM((2 * GROUPS, plan.count * PIECE, channels), jnp.float32),
            pltpu.VMEM((WL, cols, rows, channels), jnp.bfloat16),
            pltpu.SemaphoreType.DMA((len(weights),)),
            pltpu.SemaphoreType.DMA,
        ],
        input_output_aliases=aliases,
        compiler_params=pltpu.CompilerParams(vmem_limit_bytes=VMEM_LIMIT),
        cost_estimate=pl.CostEstimate(flops=24_000_000_000, bytes_accessed=20_000_000, transcendentals=8_000_000),
    )(*operands)


def per_device(
    latent,
    attention_gain,
    triple_weight,
    head_scale,
    output_weight,
    feed_gain,
    up_weight,
    down_weight,
):
    x = latent.transpose(0, 2, 1, 3)
    levels, cols, rows, channels = x.shape
    head_dim = channels // head_scale.shape[0]
    pairs = levels // WL
    lat = lax.axis_index("lat")
    count = lax.axis_size("lat")
    seam = jnp.stack([lat == 0, lat == count - 1]).astype(jnp.float32)
    factor = head_scale * (LOG2E / head_dim ** 0.5)
    plan = Plan(rows)
    bias = seam_table()
    gains = [attention_gain.reshape(1, -1), feed_gain.reshape(1, -1)]
    weights = [triple_weight, output_weight, up_weight, down_weight]

    above = from_behind(x[:, :, rows - HALF_LAT:], "lat", 1)
    below = from_behind(x[:, :, :HALF_LAT], "lat", -1)
    gap = ((0, 0), (0, 0), (0, TILE // 2 - HALF_LAT), (0, 0))
    edges = jnp.concatenate([jnp.pad(above, gap), jnp.pad(below, gap)], axis=2)

    out = None
    around = []
    for p in range(pairs):
        level = slice(WL * p, WL * p + WL)
        left, right = [
            jnp.concatenate([x[level, c], edges[level, c]], axis=2) for c in (slice(HALF_LON, cols), slice(0, HALF_LON))
        ]
        if p > 0:
            left, right, *around[-1] = lax.optimization_barrier((left, right, *around[-1]))
        around.append([from_behind(left, "lon", 1), from_behind(right, "lon", -1)])
    for p in range(pairs):
        out = block(plan, p, seam, factor, x, around[p], edges, bias, gains, weights, out)
    return out.transpose(0, 2, 1, 3)


def solution(mesh):
    in_specs = (P(None, "lat", "lon", None), P(), P(), P(), P(), P(), P(), P())
    out_specs = P(None, "lat", "lon", None)
    return jax.shard_map(
        per_device, mesh=mesh, in_specs=in_specs, out_specs=out_specs, check_vma=False
    )
```

```python
import functools

import jax
import jax.numpy as jnp
import numpy as np
from jax import lax
from jax.experimental import pallas as pl
from jax.experimental.pallas import tpu as pltpu
from jax.sharding import PartitionSpec as P

WL = 2
WLAT = 6
WLON = 12
HALF_LAT = WLAT // 2
HALF_LON = WLON // 2
EPS = 1e-05
SLABS = 4
PIECE = SLABS * WLAT
SIDE_SLABS = WL * HALF_LON
SIDE = SIDE_SLABS * WLAT
TOKENS = 2 * SIDE
GROUPS = SIDE_SLABS // SLABS
TILE = 16
THIRD = 32
LOG2E = 1.4426950408889634
VMEM_LIMIT = 44 * 1024 * 1024


def from_behind(shard, axis, by):
    count = lax.axis_size(axis)
    return lax.ppermute(shard, axis, [(i, (i + by) % count) for i in range(count)])


def norm_rows(values, gain):
    average = jnp.mean(values, axis=-1, keepdims=True)
    centred = values - average
    spread = jnp.mean(centred * centred, axis=-1, keepdims=True)
    return centred * lax.rsqrt(spread + EPS) * gain


def gelu(x):
    half = 0.5 * x
    return half + half * lax.erf(x * 0.7071067811865476)


class Plan:
    def __init__(self, rows):
        self.rows = rows
        self.count = rows // WLAT + 1
        half = rows // 2
        cut = self.count // 2
        edge = ("edge", 0, 0)
        self.picks = [
            (range(cut), [("main", 0, half), edge]),
            (range(cut, self.count - 1), [("main", half - TILE, rows)]),
            (range(self.count - 1, self.count), [("main", rows - TILE, rows), edge]),
        ]
        self.places = [(r, r + THIRD) for r in range(0, rows, THIRD)]
        self.tables = [self.pick_table(*p) for p in self.picks] + [self.place_table(*p) for p in self.places]

    def bands_of(self, r0, r1):
        return (r0 + HALF_LAT) // WLAT, (r1 - 1 + HALF_LAT) // WLAT + 1

    def pick_table(self, bands, segments):
        width = sum(SLABS * (r1 - r0 if name != "edge" else TILE) for name, r0, r1 in segments)
        table = np.zeros((len(bands) * PIECE, width), np.float32)
        for n, band in enumerate(bands):
            for s in range(SLABS):
                for i in range(WLAT):
                    r = band * WLAT - HALF_LAT + i
                    start = 0
                    for name, r0, r1 in segments:
                        span = TILE if name == "edge" else r1 - r0
                        if name != "edge" and r0 <= r < r1:
                            table[n * PIECE + s * WLAT + i, start + s * span + r - r0] = 1
                        elif name == "edge" and r < 0:
                            table[n * PIECE + s * WLAT + i, start + s * span + r + HALF_LAT] = 1
                        elif name == "edge" and r >= self.rows:
                            table[n * PIECE + s * WLAT + i, start + s * span + r - self.rows + TILE // 2] = 1
                        start += SLABS * span
        return jnp.asarray(table, jnp.bfloat16)

    def place_table(self, r0, r1):
        b0, b1 = self.bands_of(r0, r1)
        table = np.zeros((SLABS * (r1 - r0), (b1 - b0) * PIECE), np.float32)
        for s in range(SLABS):
            for r in range(r0, r1):
                band, i = divmod(r + HALF_LAT, WLAT)
                table[s * (r1 - r0) + r - r0, (band - b0) * PIECE + s * WLAT + i] = 1
        return jnp.asarray(table, jnp.bfloat16)


def seam_table():
    i = np.arange(TOKENS) % WLAT < HALF_LAT
    return jnp.asarray(np.where(i[:, None] == i[None, :], 0.0, -1e30), jnp.float32)


def gather(plan, pick_refs, main_ref, edge_of, first_col, side, dest):
    for g in range(GROUPS):
        slabs = [(s // HALF_LON, s % HALF_LON) for s in range(g * SLABS, (g + 1) * SLABS)]
        at = (side * GROUPS + g) * PIECE
        for table, (bands, segments) in zip(pick_refs, plan.picks):
            stacked = jnp.concatenate(
                [
                    edge_of(level, col) if name == "edge" else main_ref[level, first_col + col, r0:r1, :]
                    for name, r0, r1 in segments
                    for level, col in slabs
                ],
                axis=0,
            )
            picked = jnp.dot(table[...], stacked, preferred_element_type=jnp.float32)
            for n, band in enumerate(bands):
                dest[band, at:at + PIECE, :] = picked[n * PIECE:(n + 1) * PIECE]


def project_kernel(plan, *refs):
    refs = list(refs)
    own_ref, edge_ref = refs[:2]
    pick_refs = refs[2:2 + len(plan.picks)]
    gain_ref, weight_ref, xw_hbm, qkv_hbm, full_ref, xw_ref, qkv_ref, xsem, qsem = refs[2 + len(plan.picks):]
    pair = pl.program_id(0)
    for side in (0, 1):
        first = side * HALF_LON
        gather(plan, pick_refs, own_ref, lambda l, c: edge_ref[l, first + c], first, side, full_ref)
    gain = gain_ref[...]

    def copies(b):
        return (
            pltpu.make_async_copy(xw_ref.at[b], xw_hbm.at[pair, b], xsem.at[b]),
            pltpu.make_async_copy(qkv_ref.at[b], qkv_hbm.at[pair, b], qsem.at[b]),
        )

    def step(b, carry):
        values = full_ref[b]
        xw_ref[b] = values.astype(jnp.bfloat16)
        normed = norm_rows(values, gain).astype(jnp.bfloat16)
        qkv_ref[b] = jnp.dot(normed, weight_ref[...], preferred_element_type=jnp.float32).astype(jnp.bfloat16)
        for copy in copies(b):
            copy.start()
        return carry

    lax.fori_loop(0, plan.count, step, 0)

    def finish(b, carry):
        for copy in copies(b):
            copy.wait()
        return carry

    lax.fori_loop(0, plan.count, finish, 0)


def project(plan, x, edges, gain, weight):
    levels, cols, rows, channels = x.shape
    pairs = levels // WL
    whole = lambda a: pl.BlockSpec(a.shape, lambda i, n=a.ndim: (0,) * n)
    mine = lambda r: pl.BlockSpec((WL, cols, r, channels), lambda i: (i, 0, 0, 0))
    hbm = pl.BlockSpec(memory_space=pl.ANY)
    small = [*plan.tables[:len(plan.picks)], gain, weight]
    shape = lambda width: (plan.count, TOKENS, width)
    return pl.pallas_call(
        functools.partial(project_kernel, plan),
        grid=(pairs,),
        out_shape=[jax.ShapeDtypeStruct((pairs, *shape(n)), jnp.bfloat16) for n in (channels, weight.shape[1])],
        in_specs=[mine(rows), mine(TILE)] + [whole(a) for a in small],
        out_specs=[hbm, hbm],
        scratch_shapes=[
            pltpu.VMEM(shape(channels), jnp.float32),
            pltpu.VMEM(shape(channels), jnp.bfloat16),
            pltpu.VMEM(shape(weight.shape[1]), jnp.bfloat16),
            pltpu.SemaphoreType.DMA((plan.count,)),
            pltpu.SemaphoreType.DMA((plan.count,)),
        ],
        compiler_params=pltpu.CompilerParams(vmem_limit_bytes=VMEM_LIMIT),
        cost_estimate=pl.CostEstimate(flops=8_000_000_000, bytes_accessed=26_000_000, transcendentals=0),
    )(x, edges, *small)


def block_kernel(plan, pair, aliased, *refs):
    refs = list(refs)
    pop = lambda: refs.pop(0)
    seam_ref, factor_ref = pop(), pop()
    around_refs = pop(), pop()
    pick_refs = [pop() for _ in plan.picks]
    place_refs = [pop() for _ in plan.places]
    bias_ref, gain_ref, gain2_ref = pop(), pop(), pop()
    xw_hbm, mine_hbm = pop(), pop()
    weights_hbm = [pop() for _ in range(4)]
    if aliased:
        pop()
    out_ref = pop()
    weights = [pop() for _ in range(4)]
    xw_ref, mine_ref, hw_ref, att_ref, yw_ref, ow_ref, xsem, qsem, wsem, osem = refs
    qkv_ref, wo_ref, up_ref, down_ref = weights
    channels = xw_ref.shape[-1]
    heads = factor_ref.shape[0]
    head_dim = channels // heads
    group_heads = 256 // head_dim
    count = plan.count

    def arriving(b):
        return (
            pltpu.make_async_copy(xw_hbm.at[pair, b], xw_ref.at[b], xsem.at[b]),
            pltpu.make_async_copy(mine_hbm.at[pair, b], mine_ref.at[b], qsem.at[b]),
        )

    copies = [pltpu.make_async_copy(a, b, wsem.at[i]) for i, (a, b) in enumerate(zip(weights_hbm, weights))]
    copies[0].start()
    for b in range(count):
        for copy in arriving(b):
            copy.start()
        if b == 1:
            for copy in copies[1:]:
                copy.start()
    for side, ref in enumerate(around_refs):
        gather(plan, pick_refs, ref, lambda l, c: ref[l, c, plan.rows:plan.rows + TILE, :], 0, side, hw_ref)

    lane = lax.broadcasted_iota(jnp.int32, (1, 256), 1) // head_dim
    gain, gain2 = gain_ref[...], gain2_ref[...]
    copies[0].wait()

    def attend(b, bias):
        around = norm_rows(hw_ref[b], gain).astype(jnp.bfloat16)
        mine = mine_ref[b].astype(jnp.float32)
        other = jnp.dot(around, qkv_ref[:, channels:], preferred_element_type=jnp.float32)
        for g in range(heads // group_heads):
            at = g * 256
            mixed = []
            for side in (0, 1):
                rows = slice(side * SIDE, (side + 1) * SIDE)
                q = mine[rows, at:at + 256]
                k, v = [
                    jnp.concatenate(
                        [mine[rows, c * channels + at:c * channels + at + 256],
                         other[rows, (c - 1) * channels + at:(c - 1) * channels + at + 256]], axis=0
                    ).astype(jnp.bfloat16)
                    for c in (1, 2)
                ]
                stacked = jnp.concatenate([jnp.where(lane == h, q, 0.0) for h in range(group_heads)], axis=0)
                scores = lax.dot_general(
                    stacked.astype(jnp.bfloat16), k, (((1,), (1,)), ((), ())), preferred_element_type=jnp.float32
                )
                probs = []
                for h in range(group_heads):
                    s = scores[h * SIDE:(h + 1) * SIDE]
                    if bias is not None:
                        s = s + bias[:SIDE]
                    top = jnp.max(s, axis=-1, keepdims=True)
                    e = jnp.exp2((s - top) * factor_ref[g * group_heads + h])
                    probs.append(e * (1.0 / jnp.sum(e, axis=-1, keepdims=True)))
                probs = jnp.concatenate(probs, axis=0).astype(jnp.bfloat16)
                out = jnp.dot(probs, v, preferred_element_type=jnp.float32)
                total = out[:SIDE]
                for h in range(1, group_heads):
                    total = jnp.where(lane == h, out[h * SIDE:(h + 1) * SIDE], total)
                mixed.append(total)
            att_ref[b, :, at:at + 256] = jnp.concatenate(mixed, axis=0).astype(jnp.bfloat16)

    def feed(b):
        residual = xw_ref[b].astype(jnp.float32) + jnp.dot(att_ref[b], wo_ref[...], preferred_element_type=jnp.float32)
        normed = norm_rows(residual, gain2).astype(jnp.bfloat16)
        acts = gelu(jnp.dot(normed, up_ref[...], preferred_element_type=jnp.float32)).astype(jnp.bfloat16)
        result = residual + jnp.dot(acts, down_ref[...], preferred_element_type=jnp.float32)
        at = b * PIECE
        at = at if isinstance(b, int) else pl.multiple_of(at, 8)
        for g in range(2 * GROUPS):
            yw_ref[g, pl.ds(at, PIECE), :] = result[g * PIECE:(g + 1) * PIECE]

    for copy in arriving(0):
        copy.wait()
    attend(0, bias_ref[...] * seam_ref[0])
    for copy in copies[1:]:
        copy.wait()

    def step(b, carry):
        for copy in arriving(b):
            copy.wait()
        feed(b - 1)
        attend(b, None)
        return carry

    lax.fori_loop(1, count - 1, step, 0)
    for copy in arriving(count - 1):
        copy.wait()
    feed(count - 2)
    attend(count - 1, bias_ref[...] * seam_ref[1])
    feed(count - 1)

    for table, (r0, r1) in zip(place_refs, plan.places):
        b0, b1 = plan.bands_of(r0, r1)
        for g in range(2 * GROUPS):
            band_rows = yw_ref[g, b0 * PIECE:b1 * PIECE, :].astype(jnp.bfloat16)
            placed = jnp.dot(table[...], band_rows, preferred_element_type=jnp.float32).astype(jnp.bfloat16)
            for n in range(SLABS):
                s = g % GROUPS * SLABS + n
                col = s % HALF_LON + g // GROUPS * HALF_LON
                ow_ref[s // HALF_LON, col, r0:r1, :] = placed[n * THIRD:(n + 1) * THIRD]
    copy = pltpu.make_async_copy(ow_ref, out_ref.at[pl.ds(WL * pair, WL)], osem)
    copy.start()
    copy.wait()


def block(plan, pair, seam, factor, shape, around, bias, gains, own, weights, out):
    levels, cols, rows, channels = shape
    once = pl.Buffered(1)
    whole = lambda a: pl.BlockSpec(a.shape, lambda i, n=a.ndim: (0,) * n, pipeline_mode=once)
    smem = pl.BlockSpec(memory_space=pltpu.SMEM)
    hbm = pl.BlockSpec(memory_space=pl.ANY)
    small = [*around, *plan.tables, bias, *gains]
    large = [*own, *weights]
    operands = [seam, factor, *small, *large]
    specs = [smem, smem] + [whole(a) for a in small] + [hbm] * len(large)
    aliases = {}
    if out is not None:
        aliases = {len(operands): 0}
        operands.append(out)
        specs.append(hbm)
    return pl.pallas_call(
        functools.partial(block_kernel, plan, pair, out is not None),
        grid=(1,),
        out_shape=jax.ShapeDtypeStruct(shape, jnp.bfloat16),
        in_specs=specs,
        out_specs=hbm,
        scratch_shapes=[pltpu.VMEM(w.shape, w.dtype) for w in weights]
        + [
            pltpu.VMEM((plan.count, TOKENS, channels), jnp.bfloat16),
            pltpu.VMEM((plan.count, TOKENS, own[1].shape[-1]), jnp.bfloat16),
            pltpu.VMEM((plan.count, TOKENS, channels), jnp.float32),
            pltpu.VMEM((plan.count, TOKENS, channels), jnp.bfloat16),
            pltpu.VMEM((2 * GROUPS, plan.count * PIECE, channels), jnp.float32),
            pltpu.VMEM((WL, cols, rows, channels), jnp.bfloat16),
            pltpu.SemaphoreType.DMA((plan.count,)),
            pltpu.SemaphoreType.DMA((plan.count,)),
            pltpu.SemaphoreType.DMA((len(weights),)),
            pltpu.SemaphoreType.DMA,
        ],
        input_output_aliases=aliases,
        compiler_params=pltpu.CompilerParams(vmem_limit_bytes=VMEM_LIMIT),
        cost_estimate=pl.CostEstimate(flops=24_000_000_000, bytes_accessed=20_000_000, transcendentals=8_000_000),
    )(*operands)


def per_device(
    latent,
    attention_gain,
    triple_weight,
    head_scale,
    output_weight,
    feed_gain,
    up_weight,
    down_weight,
):
    x = latent.transpose(0, 2, 1, 3)
    levels, cols, rows, channels = x.shape
    head_dim = channels // head_scale.shape[0]
    pairs = levels // WL
    lat = lax.axis_index("lat")
    count = lax.axis_size("lat")
    seam = jnp.stack([lat == 0, lat == count - 1]).astype(jnp.float32)
    factor = head_scale * (LOG2E / head_dim ** 0.5)
    plan = Plan(rows)
    bias = seam_table()
    gains = [attention_gain.reshape(1, -1), feed_gain.reshape(1, -1)]
    weights = [triple_weight, output_weight, up_weight, down_weight]

    above = from_behind(x[:, :, rows - HALF_LAT:], "lat", 1)
    below = from_behind(x[:, :, :HALF_LAT], "lat", -1)
    gap = ((0, 0), (0, 0), (0, TILE // 2 - HALF_LAT), (0, 0))
    edges = jnp.concatenate([jnp.pad(above, gap), jnp.pad(below, gap)], axis=2)

    def send(p, own):
        level = slice(WL * p, WL * p + WL)
        left, right = [
            jnp.concatenate([x[level, c], edges[level, c]], axis=2) for c in (slice(HALF_LON, cols), slice(0, HALF_LON))
        ]
        if own is not None:
            left, right, *own = lax.optimization_barrier((left, right, *own))
        return [from_behind(left, "lon", 1), from_behind(right, "lon", -1)], own

    around, own = [None] * pairs, None
    around[0], _ = send(0, None)
    own = project(plan, x, edges, gains[0], triple_weight)
    for p in range(1, pairs):
        around[p], own = send(p, own)
    out = None
    for p in range(pairs):
        out = block(plan, p, seam, factor, x.shape, around[p], bias, gains, own, weights, out)
    return out.transpose(0, 2, 1, 3)


def solution(mesh):
    in_specs = (P(None, "lat", "lon", None), P(), P(), P(), P(), P(), P(), P())
    out_specs = P(None, "lat", "lon", None)
    return jax.shard_map(
        per_device, mesh=mesh, in_specs=in_specs, out_specs=out_specs, check_vma=False
    )
```

```python
import functools

import jax
import jax.numpy as jnp
import numpy as np
from jax import lax
from jax.experimental import pallas as pl
from jax.experimental.pallas import tpu as pltpu
from jax.sharding import PartitionSpec as P

WL = 2
WLAT = 6
WLON = 12
HALF_LAT = WLAT // 2
HALF_LON = WLON // 2
EPS = 1e-05
SLABS = 4
PIECE = SLABS * WLAT
SIDE_SLABS = WL * HALF_LON
SIDE = SIDE_SLABS * WLAT
TOKENS = 2 * SIDE
GROUPS = SIDE_SLABS // SLABS
TILE = 16
THIRD = 32
LOG2E = 1.4426950408889634
VMEM_LIMIT = 44 * 1024 * 1024


def from_behind(shard, axis, by):
    count = lax.axis_size(axis)
    return lax.ppermute(shard, axis, [(i, (i + by) % count) for i in range(count)])


def norm_rows(values, gain):
    average = jnp.mean(values, axis=-1, keepdims=True)
    centred = values - average
    spread = jnp.mean(centred * centred, axis=-1, keepdims=True)
    return centred * lax.rsqrt(spread + EPS) * gain


def gelu(x):
    half = 0.5 * x
    return half + half * lax.erf(x * 0.7071067811865476)


class Plan:
    def __init__(self, rows):
        self.rows = rows
        self.count = rows // WLAT + 1
        half = rows // 2
        cut = self.count // 2
        edge = ("edge", 0, 0)
        self.picks = [
            (range(cut), [("main", 0, half), edge]),
            (range(cut, self.count - 1), [("main", half - TILE, rows)]),
            (range(self.count - 1, self.count), [("main", rows - TILE, rows), edge]),
        ]
        self.places = [(r, r + THIRD) for r in range(0, rows, THIRD)]
        self.tables = [self.pick_table(*p) for p in self.picks] + [self.place_table(*p) for p in self.places]

    def bands_of(self, r0, r1):
        return (r0 + HALF_LAT) // WLAT, (r1 - 1 + HALF_LAT) // WLAT + 1

    def pick_table(self, bands, segments):
        width = sum(SLABS * (r1 - r0 if name != "edge" else TILE) for name, r0, r1 in segments)
        table = np.zeros((len(bands) * PIECE, width), np.float32)
        for n, band in enumerate(bands):
            for s in range(SLABS):
                for i in range(WLAT):
                    r = band * WLAT - HALF_LAT + i
                    start = 0
                    for name, r0, r1 in segments:
                        span = TILE if name == "edge" else r1 - r0
                        if name != "edge" and r0 <= r < r1:
                            table[n * PIECE + s * WLAT + i, start + s * span + r - r0] = 1
                        elif name == "edge" and r < 0:
                            table[n * PIECE + s * WLAT + i, start + s * span + r + HALF_LAT] = 1
                        elif name == "edge" and r >= self.rows:
                            table[n * PIECE + s * WLAT + i, start + s * span + r - self.rows + TILE // 2] = 1
                        start += SLABS * span
        return jnp.asarray(table, jnp.bfloat16)

    def place_table(self, r0, r1):
        b0, b1 = self.bands_of(r0, r1)
        table = np.zeros((SLABS * (r1 - r0), (b1 - b0) * PIECE), np.float32)
        for s in range(SLABS):
            for r in range(r0, r1):
                band, i = divmod(r + HALF_LAT, WLAT)
                table[s * (r1 - r0) + r - r0, (band - b0) * PIECE + s * WLAT + i] = 1
        return jnp.asarray(table, jnp.bfloat16)


def seam_table():
    i = np.arange(TOKENS) % WLAT < HALF_LAT
    return jnp.asarray(np.where(i[:, None] == i[None, :], 0.0, -1e30), jnp.float32)


def gather(plan, pick_refs, main_ref, edge_of, first_col, side, dest):
    for g in range(GROUPS):
        slabs = [(s // HALF_LON, s % HALF_LON) for s in range(g * SLABS, (g + 1) * SLABS)]
        at = (side * GROUPS + g) * PIECE
        for table, (bands, segments) in zip(pick_refs, plan.picks):
            stacked = jnp.concatenate(
                [
                    edge_of(level, col) if name == "edge" else main_ref[level, first_col + col, r0:r1, :]
                    for name, r0, r1 in segments
                    for level, col in slabs
                ],
                axis=0,
            )
            picked = jnp.dot(table[...], stacked, preferred_element_type=jnp.float32)
            for n, band in enumerate(bands):
                dest[band, at:at + PIECE, :] = picked[n * PIECE:(n + 1) * PIECE]


def project_kernel(plan, *refs):
    refs = list(refs)
    own_ref, edge_ref = refs[:2]
    pick_refs = refs[2:2 + len(plan.picks)]
    gain_ref, weight_ref, xw_hbm, qkv_hbm, full_ref, xw_ref, qkv_ref, xsem, qsem = refs[2 + len(plan.picks):]
    pair = pl.program_id(0)
    for side in (0, 1):
        first = side * HALF_LON
        gather(plan, pick_refs, own_ref, lambda l, c: edge_ref[l, first + c], first, side, full_ref)
    gain = gain_ref[...]

    def copies(b):
        return (
            pltpu.make_async_copy(xw_ref.at[b], xw_hbm.at[pair, b], xsem.at[b]),
            pltpu.make_async_copy(qkv_ref.at[b], qkv_hbm.at[pair, b], qsem.at[b]),
        )

    def step(b, carry):
        values = full_ref[b]
        xw_ref[b] = values.astype(jnp.bfloat16)
        normed = norm_rows(values, gain).astype(jnp.bfloat16)
        qkv_ref[b] = jnp.dot(normed, weight_ref[...], preferred_element_type=jnp.float32).astype(jnp.bfloat16)
        for copy in copies(b):
            copy.start()
        return carry

    lax.fori_loop(0, plan.count, step, 0)

    def finish(b, carry):
        for copy in copies(b):
            copy.wait()
        return carry

    lax.fori_loop(0, plan.count, finish, 0)


def project(plan, x, edges, gain, weight):
    levels, cols, rows, channels = x.shape
    pairs = levels // WL
    whole = lambda a: pl.BlockSpec(a.shape, lambda i, n=a.ndim: (0,) * n)
    mine = lambda r: pl.BlockSpec((WL, cols, r, channels), lambda i: (i, 0, 0, 0))
    hbm = pl.BlockSpec(memory_space=pl.ANY)
    small = [*plan.tables[:len(plan.picks)], gain, weight]
    shape = lambda width: (plan.count, TOKENS, width)
    return pl.pallas_call(
        functools.partial(project_kernel, plan),
        grid=(pairs,),
        out_shape=[jax.ShapeDtypeStruct((pairs, *shape(n)), jnp.bfloat16) for n in (channels, weight.shape[1])],
        in_specs=[mine(rows), mine(TILE)] + [whole(a) for a in small],
        out_specs=[hbm, hbm],
        scratch_shapes=[
            pltpu.VMEM(shape(channels), jnp.float32),
            pltpu.VMEM(shape(channels), jnp.bfloat16),
            pltpu.VMEM(shape(weight.shape[1]), jnp.bfloat16),
            pltpu.SemaphoreType.DMA((plan.count,)),
            pltpu.SemaphoreType.DMA((plan.count,)),
        ],
        compiler_params=pltpu.CompilerParams(vmem_limit_bytes=VMEM_LIMIT),
        cost_estimate=pl.CostEstimate(flops=8_000_000_000, bytes_accessed=26_000_000, transcendentals=0),
    )(x, edges, *small)


def block_kernel(plan, pair, aliased, *refs):
    refs = list(refs)
    pop = lambda: refs.pop(0)
    seam_ref, factor_ref = pop(), pop()
    around_refs = pop(), pop()
    pick_refs = [pop() for _ in plan.picks]
    place_refs = [pop() for _ in plan.places]
    bias_ref, gain_ref, gain2_ref = pop(), pop(), pop()
    xw_hbm, mine_hbm = pop(), pop()
    weights_hbm = [pop() for _ in range(4)]
    if aliased:
        pop()
    out_ref = pop()
    weights = [pop() for _ in range(4)]
    xw_ref, mine_ref, hw_ref, att_ref, yw_ref, ow_ref, xsem, qsem, wsem, osem = refs
    qkv_ref, wo_ref, up_ref, down_ref = weights
    channels = xw_ref.shape[-1]
    heads = factor_ref.shape[0]
    head_dim = channels // heads
    group_heads = 256 // head_dim
    count = plan.count

    def arriving(b):
        return (
            pltpu.make_async_copy(xw_hbm.at[pair, b], xw_ref.at[b], xsem.at[b]),
            pltpu.make_async_copy(mine_hbm.at[pair, b], mine_ref.at[b], qsem.at[b]),
        )

    copies = [pltpu.make_async_copy(a, b, wsem.at[i]) for i, (a, b) in enumerate(zip(weights_hbm, weights))]
    copies[0].start()
    for b in range(count):
        for copy in arriving(b):
            copy.start()
        if b == 1:
            for copy in copies[1:]:
                copy.start()
    for side, ref in enumerate(around_refs):
        gather(plan, pick_refs, ref, lambda l, c: ref[l, c, plan.rows:plan.rows + TILE, :], 0, side, hw_ref)

    lane = lax.broadcasted_iota(jnp.int32, (1, 256), 1) // head_dim
    gain, gain2 = gain_ref[...], gain2_ref[...]
    copies[0].wait()

    def attend(b, bias):
        around = norm_rows(hw_ref[b], gain).astype(jnp.bfloat16)
        mine = mine_ref[b].astype(jnp.float32)
        other = jnp.dot(around, qkv_ref[:, channels:], preferred_element_type=jnp.float32)
        for g in range(heads // group_heads):
            at = g * 256
            mixed = []
            for side in (0, 1):
                rows = slice(side * SIDE, (side + 1) * SIDE)
                q = mine[rows, at:at + 256]
                k, v = [
                    jnp.concatenate(
                        [mine[rows, c * channels + at:c * channels + at + 256],
                         other[rows, (c - 1) * channels + at:(c - 1) * channels + at + 256]], axis=0
                    ).astype(jnp.bfloat16)
                    for c in (1, 2)
                ]
                stacked = jnp.concatenate([jnp.where(lane == h, q, 0.0) for h in range(group_heads)], axis=0)
                scores = lax.dot_general(
                    stacked.astype(jnp.bfloat16), k, (((1,), (1,)), ((), ())), preferred_element_type=jnp.float32
                )
                probs = []
                for h in range(group_heads):
                    s = scores[h * SIDE:(h + 1) * SIDE]
                    if bias is not None:
                        s = s + bias[:SIDE]
                    top = jnp.max(s, axis=-1, keepdims=True)
                    e = jnp.exp2((s - top) * factor_ref[g * group_heads + h])
                    probs.append(e * (1.0 / jnp.sum(e, axis=-1, keepdims=True)))
                probs = jnp.concatenate(probs, axis=0).astype(jnp.bfloat16)
                out = jnp.dot(probs, v, preferred_element_type=jnp.float32)
                total = out[:SIDE]
                for h in range(1, group_heads):
                    total = jnp.where(lane == h, out[h * SIDE:(h + 1) * SIDE], total)
                mixed.append(total)
            att_ref[b, :, at:at + 256] = jnp.concatenate(mixed, axis=0).astype(jnp.bfloat16)

    def feed(b):
        residual = xw_ref[b].astype(jnp.float32) + jnp.dot(att_ref[b], wo_ref[...], preferred_element_type=jnp.float32)
        normed = norm_rows(residual, gain2).astype(jnp.bfloat16)
        acts = gelu(jnp.dot(normed, up_ref[...], preferred_element_type=jnp.float32)).astype(jnp.bfloat16)
        result = residual + jnp.dot(acts, down_ref[...], preferred_element_type=jnp.float32)
        at = b * PIECE
        at = at if isinstance(b, int) else pl.multiple_of(at, 8)
        for g in range(2 * GROUPS):
            yw_ref[g, pl.ds(at, PIECE), :] = result[g * PIECE:(g + 1) * PIECE]

    for copy in arriving(0):
        copy.wait()
    attend(0, bias_ref[...] * seam_ref[0])
    for copy in copies[1:]:
        copy.wait()

    def step(b, carry):
        for copy in arriving(b):
            copy.wait()
        feed(b - 1)
        attend(b, None)
        return carry

    lax.fori_loop(1, count - 1, step, 0)
    for copy in arriving(count - 1):
        copy.wait()
    feed(count - 2)
    attend(count - 1, bias_ref[...] * seam_ref[1])
    feed(count - 1)

    for table, (r0, r1) in zip(place_refs, plan.places):
        b0, b1 = plan.bands_of(r0, r1)
        for g in range(2 * GROUPS):
            band_rows = yw_ref[g, b0 * PIECE:b1 * PIECE, :].astype(jnp.bfloat16)
            placed = jnp.dot(table[...], band_rows, preferred_element_type=jnp.float32).astype(jnp.bfloat16)
            for n in range(SLABS):
                s = g % GROUPS * SLABS + n
                col = s % HALF_LON + g // GROUPS * HALF_LON
                ow_ref[s // HALF_LON, col, r0:r1, :] = placed[n * THIRD:(n + 1) * THIRD]
    copy = pltpu.make_async_copy(ow_ref, out_ref.at[pl.ds(WL * pair, WL)], osem)
    copy.start()
    copy.wait()


def block(plan, pair, seam, factor, shape, around, bias, gains, own, weights, out):
    levels, cols, rows, channels = shape
    once = pl.Buffered(1)
    whole = lambda a: pl.BlockSpec(a.shape, lambda i, n=a.ndim: (0,) * n, pipeline_mode=once)
    smem = pl.BlockSpec(memory_space=pltpu.SMEM)
    hbm = pl.BlockSpec(memory_space=pl.ANY)
    small = [*around, *plan.tables, bias, *gains]
    large = [*own, *weights]
    operands = [seam, factor, *small, *large]
    specs = [smem, smem] + [whole(a) for a in small] + [hbm] * len(large)
    aliases = {}
    if out is not None:
        aliases = {len(operands): 0}
        operands.append(out)
        specs.append(hbm)
    return pl.pallas_call(
        functools.partial(block_kernel, plan, pair, out is not None),
        grid=(1,),
        out_shape=jax.ShapeDtypeStruct(shape, jnp.bfloat16),
        in_specs=specs,
        out_specs=hbm,
        scratch_shapes=[pltpu.VMEM(w.shape, w.dtype) for w in weights]
        + [
            pltpu.VMEM((plan.count, TOKENS, channels), jnp.bfloat16),
            pltpu.VMEM((plan.count, TOKENS, own[1].shape[-1]), jnp.bfloat16),
            pltpu.VMEM((plan.count, TOKENS, channels), jnp.float32),
            pltpu.VMEM((plan.count, TOKENS, channels), jnp.bfloat16),
            pltpu.VMEM((2 * GROUPS, plan.count * PIECE, channels), jnp.float32),
            pltpu.VMEM((WL, cols, rows, channels), jnp.bfloat16),
            pltpu.SemaphoreType.DMA((plan.count,)),
            pltpu.SemaphoreType.DMA((plan.count,)),
            pltpu.SemaphoreType.DMA((len(weights),)),
            pltpu.SemaphoreType.DMA,
        ],
        input_output_aliases=aliases,
        compiler_params=pltpu.CompilerParams(vmem_limit_bytes=VMEM_LIMIT),
        cost_estimate=pl.CostEstimate(flops=24_000_000_000, bytes_accessed=20_000_000, transcendentals=8_000_000),
    )(*operands)


def per_device(
    latent,
    attention_gain,
    triple_weight,
    head_scale,
    output_weight,
    feed_gain,
    up_weight,
    down_weight,
):
    x = latent.transpose(0, 2, 1, 3)
    levels, cols, rows, channels = x.shape
    head_dim = channels // head_scale.shape[0]
    pairs = levels // WL
    lat = lax.axis_index("lat")
    count = lax.axis_size("lat")
    seam = jnp.stack([lat == 0, lat == count - 1]).astype(jnp.float32)
    factor = head_scale * (LOG2E / head_dim ** 0.5)
    plan = Plan(rows)
    bias = seam_table()
    gains = [attention_gain.reshape(1, -1), feed_gain.reshape(1, -1)]
    weights = [triple_weight, output_weight, up_weight, down_weight]

    above = from_behind(x[:, :, rows - HALF_LAT:], "lat", 1)
    below = from_behind(x[:, :, :HALF_LAT], "lat", -1)
    gap = ((0, 0), (0, 0), (0, TILE // 2 - HALF_LAT), (0, 0))
    edges = jnp.concatenate([jnp.pad(above, gap), jnp.pad(below, gap)], axis=2)

    def send(p, own):
        source = (x, edges)
        if own is not None:
            *source, own[0], own[1] = lax.optimization_barrier((x, edges, *own))
        level = slice(WL * p, WL * p + WL)
        left, right = [
            jnp.concatenate([a[level, c] for a in source], axis=2) for c in (slice(HALF_LON, cols), slice(0, HALF_LON))
        ]
        return [from_behind(left, "lon", 1), from_behind(right, "lon", -1)], own

    around, own = [None] * pairs, None
    around[0], _ = send(0, None)
    own = list(project(plan, x, edges, gains[0], triple_weight))
    for p in range(1, pairs):
        around[p], own = send(p, own)
    out = None
    for p in range(pairs):
        out = block(plan, p, seam, factor, x.shape, around[p], bias, gains, own, weights, out)
    return out.transpose(0, 2, 1, 3)


def solution(mesh):
    in_specs = (P(None, "lat", "lon", None), P(), P(), P(), P(), P(), P(), P())
    out_specs = P(None, "lat", "lon", None)
    return jax.shard_map(
        per_device, mesh=mesh, in_specs=in_specs, out_specs=out_specs, check_vma=False
    )
```
